256 devices in a mesh: leaf: 4 (over y), row: 16 (over x_lo, z), col: 4 (over x_hi, core).
Axes of the slice: x: 4 (x_hi: 2, x_lo: 2; x = x_hi * 2 + x_lo), y: 4, z: 8, core: 2. Of those that a mesh axis runs over, the one named last changes fastest.
Arguments:
- ancestor_cols: bfloat16 [16, 4, 512, 32768], P(None, 'col', 'leaf', 'row'), may hold values from -6 to 6
- factor: bfloat16 [4, 32768, 256], P('leaf', ('row', 'col')), may hold values from -0.046875 to 0.046875
- block_mask: int32 [4, 128], P('leaf'), may hold values 0 or 1
- diag_inverse: float32 [4, 256, 256], P('leaf'), may hold values from -6 to 6
Outputs:
- inverse_cols: bfloat16 [4, 32768, 256], P('leaf', ('row', 'col'))
- diag_block: float32 [4, 256, 256], P('leaf')
The draws below stay inside these ranges and needn't reach their ends.
All inputs are finite; a program needn't handle non-finite values. No bound on the sum of `block_mask` on one device may be relied on, other than what follows from the above.
Results may differ from the reference program's by a relative error of at most 0.0021.
Values may be sent and summed in bfloat16 or wider, within the bound.
No kernel may reach another device: no remote copies, remote signals or barrier semaphores. Data moves between devices by JAX's collectives and lax.ppermute only.
A program may use at most 128 MiB of HBM per device.

```python
import jax
import jax.numpy as jnp
from jax import lax

M = 32768
W = 256
NK_ALL = 4
NB = 128
SUBQ = 512
N_ROW = 16
N_COL = 4


def with_ends(array, own_key, smallest, top_value):
    shape = array.shape
    place = [jax.random.randint(jax.random.fold_in(own_key, axis), (), 0, shape[axis]) for axis in range(len(shape))]
    array = array.at[tuple(place)].set(smallest)
    longest = shape.index(max(shape))
    place[longest] = (place[longest] + 1) % shape[longest]
    return array.at[tuple(place)].set(top_value)


def levels(key, shape, pieces, least, top_value):
    def one(dim, parts):
        draws = jax.random.uniform(jax.random.fold_in(jax.random.fold_in(key, 6), dim), (parts,), jnp.float32, least / len(pieces), top_value / len(pieces))
        return jnp.repeat(jnp.exp(draws), shape[dim] // parts).reshape((-1,) + (1,) * (len(shape) - dim - 1))

    gain = one(*pieces[0])
    for cut in pieces[1:]:
        gain = gain * one(*cut)
    return gain


def normal_values(key, extent, width, bound, shards=(), kind=jnp.bfloat16):
    entries = width * jax.random.normal(key, extent, jnp.float32)
    if shards:
        entries = entries * levels(key, extent, shards, -0.22, 0.18)
    return jnp.clip(entries, -bound, bound).astype(kind)


def setup_inputs(seed: int = 0) -> dict:
    splits = jax.random.split(jax.random.key(seed), 5)
    ancestor_cols = normal_values(splits[0], (N_ROW, N_COL, SUBQ, M), 1.0, 6.0, ((1, 4), (2, 4), (3, 16)))
    factor = normal_values(splits[1], (NK_ALL, M, W), (M // 2) ** -0.5, 0.046875, ((0, 4), (1, 64)))
    block_mask = with_ends((jax.random.randint(splits[2], (NK_ALL, NB), 0, 2) < 1).astype(jnp.int32), jax.random.fold_in(splits[2], 1), 0, 1)
    diag_inverse = normal_values(splits[3], (NK_ALL, W, W), 1.0, 6.0, ((0, 4),), jnp.float32)
    return dict(ancestor_cols=ancestor_cols, factor=factor, block_mask=block_mask, diag_inverse=diag_inverse)


def reference(ancestor_cols, factor, block_mask, diag_inverse):
    flat = ancestor_cols.reshape(M, M)
    live = jnp.repeat(block_mask, W, axis=1).astype(factor.dtype)
    masked = factor * live[:, :, None]
    stacked = jnp.transpose(masked, (1, 0, 2)).reshape(M, NK_ALL * W)
    product = lax.dot_general(flat, stacked, (((0,), (0,)), ((), ())), preferred_element_type=jnp.float32)
    product = jnp.transpose(product.reshape(M, NK_ALL, W), (1, 0, 2))
    inverse_cols = (-product).astype(jnp.bfloat16)
    terms = jnp.einsum("kjw,kjv->kwv", masked.astype(jnp.float32), inverse_cols.astype(jnp.float32))
    diag_block = diag_inverse - terms
    return inverse_cols, diag_block
```

```python
import jax
import jax.numpy as jnp
from jax import lax
from jax.sharding import Mesh, PartitionSpec as P

AXES = ("y", "xlo", "z", "xhi", "core")
ROW = ("xlo", "z")
COL = ("xhi", "core")
ALONG_X = ("xlo", "xhi", "core")
F32 = jnp.float32
BF16 = jnp.bfloat16


def ring_pairs(num):
    return [(2 * z + c, 2 * ((z + (1 if c == 0 else -1)) % num) + c) for z in range(num) for c in range(2)]


SWAP = [(0, 1), (1, 0)]


def shards(ancestor_cols, factor, block_mask, diag_inverse):
    num_z = lax.axis_size("z")
    num_y = lax.axis_size("y")
    quarter = ancestor_cols.shape[2]
    height = ancestor_cols.shape[3]
    width = factor.shape[2]
    sub = factor.shape[1]
    z = lax.axis_index("z")
    core = lax.axis_index("core")
    group = (lax.axis_index("xlo") * num_z + z) * 4 + lax.axis_index("xhi") * 2 + core
    per = sub // width
    live = lax.dynamic_slice_in_dim(block_mask[0], group * per, per, 0)
    masked = (factor.reshape(per, width, width) * live[:, None, None].astype(BF16)).reshape(sub, width)

    pieces = jnp.broadcast_to(masked.reshape(num_y, 1, quarter, width), (num_y, 2, quarter, width))
    own = lax.all_to_all(pieces.reshape(num_y * 2, quarter, width), ("y", "xlo"), 0, 0)
    other = lax.ppermute(own, "core", SWAP)
    blocks = ancestor_cols.reshape(2, num_z, quarter, height)
    step = jnp.where(core == 0, 1, -1)

    def term(rows, where):
        cols = lax.dynamic_index_in_dim(blocks, jnp.remainder(where, num_z), 1, keepdims=False)
        return jnp.einsum(
            "xti,kxtw->kiw", cols, rows.reshape(num_y, 2, quarter, width), preferred_element_type=F32
        )

    partial = term(own, z)
    both = jnp.concatenate([own[None], other[None]], 0)
    pairs = ring_pairs(num_z)
    for hop in range(1, num_z // 2):
        both = lax.ppermute(both, ("z", "core"), pairs)
        swapped = lax.ppermute(both[1], "core", SWAP)
        partial = partial + term(both[0], z - step * hop) + term(swapped, z + step * hop)
    last = lax.ppermute(both[0], ("z", "core"), pairs)
    partial = partial + term(last, z + num_z // 2)

    halves = partial.reshape(num_y, 2, 2, sub, width)
    keep = lax.dynamic_index_in_dim(halves, core, 2, keepdims=False)
    give = lax.dynamic_index_in_dim(halves, 1 - core, 2, keepdims=False)
    summed = keep + lax.ppermute(give, "core", SWAP)
    parts = lax.all_to_all(summed.reshape(num_y * 2, sub, width), ("y", "xhi"), 0, 0)
    inverse_cols = (-jnp.sum(parts, 0)).astype(BF16)

    product = jnp.einsum("jw,jv->wv", masked, inverse_cols, preferred_element_type=F32)
    split = product.reshape(8, width // 8, width)
    mine = jnp.sum(lax.all_to_all(split, ALONG_X, 0, 0), 0)
    over_z = jnp.sum(lax.all_to_all(jnp.broadcast_to(mine, (num_z,) + mine.shape), "z", 0, 0), 0)
    total = lax.all_to_all(jnp.broadcast_to(over_z, (8,) + over_z.shape), ALONG_X, 0, 0)
    return inverse_cols[None], diag_inverse - total.reshape(1, width, width)


def solution(mesh):
    fine = Mesh(mesh.devices.reshape(4, 2, 8, 2, 2), AXES)
    rows = ROW + COL
    in_specs = (P(None, COL, "y", ROW), P("y", rows, None), P("y", None), P("y", None, None))
    out_specs = (P("y", rows, None), P("y", None, None))
    return jax.shard_map(shards, mesh=fine, in_specs=in_specs, out_specs=out_specs, check_vma=False)
```

```python
import functools

import jax
import jax.numpy as jnp
from jax import lax
from jax.experimental import pallas as pl
from jax.experimental.pallas import tpu as pltpu
from jax.sharding import Mesh, PartitionSpec as P

AXES = ("y", "xlo", "z", "xhi", "core")
ROW = ("xlo", "z")
COL = ("xhi", "core")
ALONG_X = ("xlo", "xhi", "core")
F32 = jnp.float32
F16 = jnp.float16
BF16 = jnp.bfloat16
SWAP = [(0, 1), (1, 0)]
VMEM = 48 * 2**20


def products(cols, rows):
    turned = [c[...].reshape(-1, c.shape[-1]).T for c in cols]
    kids = sum(r.shape[0] for r in rows[0])
    out = []
    for k in range(kids):
        total = None
        for t, group in zip(turned, rows):
            part, at = group[0], k
            if at >= part.shape[0]:
                at -= part.shape[0]
                part = group[1]
            d = jnp.dot(t, part[at], preferred_element_type=F32)
            total = d if total is None else total + d
        out.append(total)
    return out


def add_kernel(num, more, where_ref, *refs):
    cols, rows = refs[:num], [[r] for r in refs[num : 2 * num]]
    out_ref = refs[-1]
    for k, value in enumerate(products(cols, rows)):
        out_ref[k] = refs[2 * num][k] + value if more else value


def add_blocks(blocks, where, rows, partial=None):
    num, tile = len(rows), 512
    kids, _, width = rows[0].shape
    _, _, quarter, height = blocks.shape
    cost = 2 * num * 2 * quarter * height * kids * width
    moved = num * (blocks.nbytes // 8 + rows[0].nbytes) + kids * height * width * 4 * (1 if partial is None else 2)
    own = pl.BlockSpec((kids, tile, width), lambda i, w: (0, i, 0))
    return pl.pallas_call(
        functools.partial(add_kernel, num, partial is not None),
        out_shape=jax.ShapeDtypeStruct((kids, height, width), F32),
        grid_spec=pltpu.PrefetchScalarGridSpec(
            num_scalar_prefetch=1,
            grid=(height // tile,),
            in_specs=[
                pl.BlockSpec((2, 1, quarter, tile), lambda i, w, b=b: (0, w[b], 0, i)) for b in range(num)
            ]
            + [pl.BlockSpec(r.shape, lambda i, w: (0, 0, 0)) for r in rows]
            + ([] if partial is None else [own]),
            out_specs=own,
        ),
        input_output_aliases={} if partial is None else {1 + 2 * num: 0},
        compiler_params=pltpu.CompilerParams(vmem_limit_bytes=VMEM),
        cost_estimate=pl.CostEstimate(flops=cost, bytes_accessed=moved, transcendentals=0),
        name="add_blocks",
    )(where, *([blocks] * num), *rows, *([] if partial is None else [partial]))


def half_kernel(where_ref, col_ref, low_ref, high_ref, partial_ref, out_ref, top_ref):
    @pl.when((pl.program_id(0) == 0) & (pl.program_id(1) == 0))
    def _():
        top_ref[...] = jnp.zeros_like(top_ref)

    top = top_ref[...]
    for k, value in enumerate(products([col_ref], [[low_ref, high_ref]])):
        value = partial_ref[k] + value
        out_ref[k, 0] = value
        top = jnp.maximum(top, jnp.max(jnp.abs(value).reshape(-1, *top.shape), axis=0))
    top_ref[...] = top


def finish_half(blocks, where, low, high, partial):
    tile = 256
    _, _, quarter, height = blocks.shape
    kids, _, width = partial.shape
    per = height // 4 // tile
    return pl.pallas_call(
        half_kernel,
        out_shape=(
            jax.ShapeDtypeStruct((kids, 2, height // 4, width), F32),
            jax.ShapeDtypeStruct((8, width), F32),
        ),
        grid_spec=pltpu.PrefetchScalarGridSpec(
            num_scalar_prefetch=1,
            grid=(2, per),
            in_specs=[
                pl.BlockSpec((2, 1, quarter, tile), lambda h, i, w: (0, w[0], 0, (h * 2 + w[1]) * per + i)),
                pl.BlockSpec(low.shape, lambda h, i, w: (0, 0, 0)),
                pl.BlockSpec(high.shape, lambda h, i, w: (0, 0, 0)),
                pl.BlockSpec((kids, tile, width), lambda h, i, w: (0, (h * 2 + w[1]) * per + i, 0)),
            ],
            out_specs=(
                pl.BlockSpec((kids, 1, tile, width), lambda h, i, w: (0, h, i, 0)),
                pl.BlockSpec((8, width), lambda h, i, w: (0, 0)),
            ),
        ),
        compiler_params=pltpu.CompilerParams(vmem_limit_bytes=VMEM),
        cost_estimate=pl.CostEstimate(
            flops=2 * 2 * quarter * (height // 2) * kids * width,
            bytes_accessed=blocks.nbytes // 16 + partial.nbytes,
            transcendentals=0,
        ),
        name="finish_half",
    )(where, blocks, low, high, partial)


def shards(ancestor_cols, factor, block_mask, diag_inverse):
    num_z = lax.axis_size("z")
    num_y = lax.axis_size("y")
    quarter = ancestor_cols.shape[2]
    height = ancestor_cols.shape[3]
    width = factor.shape[2]
    sub = factor.shape[1]
    z = lax.axis_index("z")
    core = lax.axis_index("core")
    group = (lax.axis_index("xlo") * num_z + z) * 4 + lax.axis_index("xhi") * 2 + core
    per = sub // width
    live = lax.dynamic_slice_in_dim(block_mask[0], group * per, per, 0)
    masked = (factor.reshape(per, width, width) * live[:, None, None].astype(BF16)).reshape(sub, width)
    blocks = ancestor_cols.reshape(2, num_z, quarter, height)

    pieces = jnp.broadcast_to(masked.reshape(num_y, 1, quarter, width), (num_y, 2, quarter, width))
    own = lax.all_to_all(pieces.reshape(num_y * 2, quarter, width), ("y", "xlo"), 0, 0)
    own = own.reshape(num_y, 2 * quarter, width)

    up = [(i, (i + 1) % num_z) for i in range(num_z)]
    down = [(i, (i - 1) % num_z) for i in range(num_z)]

    def at(*offsets):
        return jnp.stack([jnp.remainder(z + o, num_z) for o in offsets]).astype(jnp.int32)

    below, above = lax.ppermute(own, "z", up), lax.ppermute(own, "z", down)
    below2, above2 = lax.ppermute(below, "z", up), lax.ppermute(above, "z", down)
    partial = add_blocks(blocks, at(0, -1, 1), [own, below, above])
    below3, above3 = lax.ppermute(below2, "z", up), lax.ppermute(above2, "z", down)
    partial = add_blocks(blocks, at(-2, 2), [below2, above2], partial)
    half = num_y // 2
    low, high = lax.ppermute(below3[:half], "z", up), lax.ppermute(above3[half:], "z", down)
    partial = add_blocks(blocks, at(-3, 3), [below3, above3], partial)

    far = jnp.remainder(z + 4, num_z)
    give, give_top = finish_half(blocks, jnp.stack([far, 1 - core]).astype(jnp.int32), low, high, partial)
    got, got_top = lax.ppermute(give, "core", SWAP), lax.ppermute(give_top, "core", SWAP)
    keep, keep_top = finish_half(blocks, jnp.stack([far, core]).astype(jnp.int32), low, high, partial)

    bound = jnp.maximum(jnp.max(keep_top) + jnp.max(got_top), 2.0**-100)
    power = jnp.ceil(jnp.log2(bound)) + 1.0
    scaled = ((keep + got) * jnp.exp2(15.0 - power)).astype(F16).reshape(num_y * 2, sub, width)
    tail = jnp.broadcast_to(power.astype(F16), (num_y * 2, 16, width))
    parts = lax.all_to_all(jnp.concatenate([scaled, tail], 1), ("y", "xhi"), 0, 0)
    back = jnp.exp2(parts[:, sub, 0].astype(F32) - 15.0)
    total = jnp.sum(parts[:, :sub].astype(F32) * back[:, None, None], 0)
    inverse_cols = (-total).astype(BF16)

    product = jnp.einsum("jw,jv->wv", masked, inverse_cols, preferred_element_type=F32)
    split = product.reshape(8, width // 8, width)
    mine = jnp.sum(lax.all_to_all(split, ALONG_X, 0, 0), 0)
    over_z = jnp.sum(lax.all_to_all(jnp.broadcast_to(mine, (num_z,) + mine.shape), "z", 0, 0), 0)
    whole = lax.all_to_all(jnp.broadcast_to(over_z, (8,) + over_z.shape), ALONG_X, 0, 0)
    return inverse_cols[None], diag_inverse - whole.reshape(1, width, width)


def solution(mesh):
    fine = Mesh(mesh.devices.reshape(4, 2, 8, 2, 2), AXES)
    rows = ROW + COL
    in_specs = (P(None, COL, "y", ROW), P("y", rows, None), P("y", None), P("y", None, None))
    out_specs = (P("y", rows, None), P("y", None, None))
    return jax.shard_map(shards, mesh=fine, in_specs=in_specs, out_specs=out_specs, check_vma=False)
```

```python
import functools

import jax
import jax.numpy as jnp
from jax import lax
from jax.experimental import pallas as pl
from jax.experimental.pallas import tpu as pltpu
from jax.sharding import Mesh, PartitionSpec as P

AXES = ("y", "xlo", "z", "xhi", "core")
ROW = ("xlo", "z")
COL = ("xhi", "core")
ALONG_X = ("xlo", "xhi", "core")
F32 = jnp.float32
F16 = jnp.float16
BF16 = jnp.bfloat16
SWAP = [(0, 1), (1, 0)]
TILE = 512


def turn_kernel(cols_ref, out_ref):
    out_ref[0] = cols_ref[...].reshape(-1, cols_ref.shape[-1]).T


def turn(blocks):
    pair, num, quarter, height = blocks.shape
    tile = 512
    return pl.pallas_call(
        turn_kernel,
        out_shape=jax.ShapeDtypeStruct((num, height, pair * quarter), BF16),
        grid=(num, height // tile),
        in_specs=[pl.BlockSpec((pair, 1, quarter, tile), lambda z, i: (0, z, 0, i))],
        out_specs=pl.BlockSpec((1, tile, pair * quarter), lambda z, i: (z, i, 0)),
        compiler_params=pltpu.CompilerParams(vmem_limit_bytes=16 * 2**20),
        cost_estimate=pl.CostEstimate(flops=0, bytes_accessed=2 * blocks.nbytes, transcendentals=0),
        name="turn",
    )(blocks)


def half_kernel(num, more, where_ref, turned_ref, *refs):
    rows, (out_ref, held, sems) = refs[:num], refs[-3:]
    kids, _, sub, _ = out_ref.shape
    per = sub // TILE

    def copy(c):
        begin = pl.multiple_of((2 * (c // per) + where_ref[num]) * sub + (c % per) * TILE, TILE)
        blocks = pl.ds(where_ref[0], 1) if num == 1 else slice(None)
        return pltpu.make_async_copy(turned_ref.at[blocks, pl.ds(begin, TILE)], held.at[c], sems.at[c])

    for c in range(2 * per):
        copy(c).start()

    @pl.loop(0, 2 * per)
    def _(c):
        copy(c).wait()
        here = pl.ds(pl.multiple_of((c % per) * TILE, TILE), TILE)
        cols = [held[c, 0 if num == 1 else where_ref[b]] for b in range(num)]
        cols = jnp.concatenate(cols, 1)
        for k in range(kids):
            value = jnp.dot(cols, jnp.concatenate([r[k] for r in rows], 0), preferred_element_type=F32)
            out_ref[k, c // per, here] = refs[num][k, c // per, here] + value if more else value


def half_product(turned, where, rows, partial=None):
    num = len(rows)
    count, height, depth = turned.shape
    kids, _, width = rows[0].shape
    sub = height // 4
    more = [] if partial is None else [partial]
    chunks = 2 * sub // TILE
    return pl.pallas_call(
        functools.partial(half_kernel, num, bool(more)),
        out_shape=jax.ShapeDtypeStruct((kids, 2, sub, width), F32),
        in_specs=[pl.BlockSpec(memory_space=pltpu.SMEM), pl.BlockSpec(memory_space=pl.ANY)]
        + [pl.BlockSpec(memory_space=pltpu.VMEM)] * (len(rows) + len(more)),
        out_specs=pl.BlockSpec(memory_space=pltpu.VMEM),
        scratch_shapes=[
            pltpu.VMEM((chunks, 1 if num == 1 else count, TILE, depth), BF16),
            pltpu.SemaphoreType.DMA((chunks,)),
        ],
        input_output_aliases={2 + len(rows): 0} if more else {},
        compiler_params=pltpu.CompilerParams(vmem_limit_bytes=20 * 2**20),
        cost_estimate=pl.CostEstimate(
            flops=num * depth * height * kids * width,
            bytes_accessed=num * depth * height + kids * height * width * 2 * (1 + len(more)),
            transcendentals=0,
        ),
        name="half_product",
    )(where, turned, *rows, *more)


def pair_kernel(keep_ref, got_ref, message_ref):
    sub, width = keep_ref.shape[2:]
    both = keep_ref[0, 0] + got_ref[0, 0]
    top = jnp.max(jnp.max(jnp.abs(both).reshape(-1, 8, width), axis=0), axis=(0, 1), keepdims=True)
    power = jnp.ceil(jnp.log2(jnp.maximum(top, 2.0**-100))) + 1.0
    message_ref[0, :sub] = both * jnp.exp2(15.0 - power)
    message_ref[0, sub:] = jnp.broadcast_to(power, (message_ref.shape[1] - sub, width))


def add_pair(keep, got):
    kids, halves, sub, width = keep.shape
    spec = pl.BlockSpec((1, 1, sub, width), lambda k, h: (k, h, 0, 0))
    return pl.pallas_call(
        pair_kernel,
        out_shape=jax.ShapeDtypeStruct((kids * halves, sub + 16, width), F32),
        grid=(kids, halves),
        in_specs=[spec, spec],
        out_specs=pl.BlockSpec((1, sub + 16, width), lambda k, h: (k * halves + h, 0, 0)),
        compiler_params=pltpu.CompilerParams(vmem_limit_bytes=16 * 2**20),
        cost_estimate=pl.CostEstimate(flops=keep.size * 4, bytes_accessed=3 * keep.nbytes, transcendentals=0),
        name="add_pair",
    )(keep, got)


def shards(ancestor_cols, factor, block_mask, diag_inverse):
    num_z = lax.axis_size("z")
    num_y = lax.axis_size("y")
    quarter = ancestor_cols.shape[2]
    height = ancestor_cols.shape[3]
    width = factor.shape[2]
    sub = factor.shape[1]
    z = lax.axis_index("z")
    core = lax.axis_index("core")
    group = (lax.axis_index("xlo") * num_z + z) * 4 + lax.axis_index("xhi") * 2 + core
    per = sub // width
    live = lax.dynamic_slice_in_dim(block_mask[0], group * per, per, 0)
    masked = (factor.reshape(per, width, width) * live[:, None, None].astype(BF16)).reshape(sub, width)
    blocks = ancestor_cols.reshape(2, num_z, quarter, height)

    order = [jnp.remainder(z + o, num_z) for o in (0, -1, 1, -2, 2, -3, 3, num_z // 2)]
    first, last, every = order[:7] + [1 - core], order[7:] + [1 - core], order + [core]
    first, last, every = (jnp.stack(w).astype(jnp.int32) for w in (first, last, every))

    pieces = jnp.broadcast_to(masked.reshape(num_y, 1, quarter, width), (num_y, 2, quarter, width))
    pieces, first, last, every = lax.optimization_barrier((pieces, first, last, every))
    own = lax.all_to_all(pieces.reshape(num_y * 2, quarter, width), ("y", "xlo"), 0, 0)
    own = own.reshape(num_y, 2 * quarter, width)

    up = [(i, (i + 1) % num_z) for i in range(num_z)]
    down = [(i, (i - 1) % num_z) for i in range(num_z)]
    below, above = lax.ppermute(own, "z", up), lax.ppermute(own, "z", down)
    below, above, turned = lax.optimization_barrier((below, above, turn(blocks)))
    below2, above2 = lax.ppermute(below, "z", up), lax.ppermute(above, "z", down)
    below3, above3 = lax.ppermute(below2, "z", up), lax.ppermute(above2, "z", down)
    far = lax.ppermute(below3, "z", up)

    near = [own, below, above, below2, above2, below3, above3]
    partial = half_product(turned, first, near)
    give = half_product(turned, last, [far], partial)
    got = lax.ppermute(give, "core", SWAP)
    keep = half_product(turned, every, near + [far])

    parts = lax.all_to_all(add_pair(keep, got).astype(F16), ("y", "xhi"), 0, 0)
    back = jnp.exp2(parts[:, sub, 0].astype(F32) - 15.0)
    total = jnp.sum(parts[:, :sub].astype(F32) * back[:, None, None], 0)
    inverse_cols = lax.optimization_barrier((-total).astype(BF16))

    product = jnp.einsum("jw,jv->wv", masked, inverse_cols, preferred_element_type=F32)
    split = product.reshape(8, width // 8, width)
    mine = jnp.sum(lax.all_to_all(split, ALONG_X, 0, 0), 0)
    over_z = jnp.sum(lax.all_to_all(jnp.broadcast_to(mine, (num_z,) + mine.shape), "z", 0, 0), 0)
    whole = lax.all_to_all(jnp.broadcast_to(over_z, (8,) + over_z.shape), ALONG_X, 0, 0)
    return inverse_cols[None], diag_inverse - whole.reshape(1, width, width)


def solution(mesh):
    fine = Mesh(mesh.devices.reshape(4, 2, 8, 2, 2), AXES)
    rows = ROW + COL
    in_specs = (P(None, COL, "y", ROW), P("y", rows, None), P("y", None), P("y", None, None))
    out_specs = (P("y", rows, None), P("y", None, None))
    return jax.shard_map(shards, mesh=fine, in_specs=in_specs, out_specs=out_specs, check_vma=False)
```

```python
import functools

import jax
import jax.numpy as jnp
from jax import lax
from jax.experimental import pallas as pl
from jax.experimental.pallas import tpu as pltpu
from jax.sharding import Mesh, PartitionSpec as P

AXES = ("y", "xlo", "z", "xhi", "core")
ROW = ("xlo", "z")
COL = ("xhi", "core")
ALONG_X = ("xlo", "xhi", "core")
F32 = jnp.float32
F16 = jnp.float16
BF16 = jnp.bfloat16
SWAP = [(0, 1), (1, 0)]
def mask_kernel(place_ref, mask_ref, factor_ref, pieces_ref, masked_ref):
    pair, quarter = pieces_ref.shape[1:3]
    width = factor_ref.shape[2]
    for k in range(pieces_ref.shape[0]):
        block = place_ref[0] + k * quarter // width
        part = factor_ref[0, k * quarter : (k + 1) * quarter]
        part = jnp.where(mask_ref[0, block] != 0, part, jnp.zeros_like(part))
        masked_ref[k * quarter : (k + 1) * quarter] = part
        for x in range(pair):
            pieces_ref[k, x] = part


def mask(place, block_mask, factor, quarter):
    _, sub, width = factor.shape
    return pl.pallas_call(
        mask_kernel,
        out_shape=(
            jax.ShapeDtypeStruct((sub // quarter, 2, quarter, width), BF16),
            jax.ShapeDtypeStruct((sub, width), BF16),
        ),
        in_specs=[pl.BlockSpec(memory_space=pltpu.SMEM)] * 2 + [pl.BlockSpec(memory_space=pltpu.VMEM)],
        out_specs=tuple([pl.BlockSpec(memory_space=pltpu.VMEM)] * 2),
        cost_estimate=pl.CostEstimate(flops=factor.size, bytes_accessed=4 * factor.nbytes, transcendentals=0),
        name="mask",
    )(place, block_mask, factor)


def turn_kernel(cols_ref, out_ref):
    out_ref[0] = cols_ref[...].reshape(-1, cols_ref.shape[-1]).T


def turn(blocks):
    pair, num, quarter, height = blocks.shape
    tile = 512
    return pl.pallas_call(
        turn_kernel,
        out_shape=jax.ShapeDtypeStruct((num, height, pair * quarter), BF16),
        grid=(num, height // tile),
        in_specs=[pl.BlockSpec((pair, 1, quarter, tile), lambda z, i: (0, z, 0, i))],
        out_specs=pl.BlockSpec((1, tile, pair * quarter), lambda z, i: (z, i, 0)),
        compiler_params=pltpu.CompilerParams(vmem_limit_bytes=16 * 2**20),
        cost_estimate=pl.CostEstimate(flops=0, bytes_accessed=2 * blocks.nbytes, transcendentals=0),
        name="turn",
    )(blocks)


def rows_of(where_ref, half, sub):
    return pl.ds(pl.multiple_of((2 * half + where_ref[where_ref.shape[0] - 1]) * sub, sub), sub)


def pick_kernel(where_ref, turned_ref, out_ref):
    for b in range(out_ref.shape[0]):
        for h in range(2):
            out_ref[b, h] = turned_ref[where_ref[b], rows_of(where_ref, h, out_ref.shape[2])]


def pick(turned, where):
    _, height, depth = turned.shape
    num = where.shape[0] - 1
    return pl.pallas_call(
        pick_kernel,
        out_shape=jax.ShapeDtypeStruct((num, 2, height // 4, depth), BF16),
        in_specs=[pl.BlockSpec(memory_space=pltpu.SMEM), pl.BlockSpec(memory_space=pltpu.VMEM)],
        out_specs=pl.BlockSpec(memory_space=pltpu.VMEM),
        compiler_params=pltpu.CompilerParams(vmem_limit_bytes=16 * 2**20),
        cost_estimate=pl.CostEstimate(flops=0, bytes_accessed=2 * num * height * depth, transcendentals=0),
        name="pick",
    )(where, turned)


def half_kernel(num, spare, more, where_ref, turned_ref, *refs):
    rows, out_ref = refs[: num + len(spare)], refs[-1]
    parts_ref = refs[num + len(spare)] if spare else None
    kids, _, sub, _ = out_ref.shape
    for h in range(2):
        here = rows_of(where_ref, h, sub)
        cols = [turned_ref[where_ref[b], here] for b in range(num)] + [parts_ref[p, h] for p in spare]
        cols = jnp.concatenate(cols, 1)
        for k in range(kids):
            value = jnp.dot(cols, jnp.concatenate([r[k] for r in rows], 0), preferred_element_type=F32)
            out_ref[k, h] = refs[-2][k, h] + value if more else value


def half_product(turned, where, rows, partial=None, parts=None, spare=(), others=(), weight=1):
    num = len(rows)
    _, height, depth = turned.shape
    kids, _, width = rows[0].shape
    more = [] if partial is None else [partial]
    extra = [parts] if spare else []
    arrays = [turned, *rows, *others, *extra, *more]
    return pl.pallas_call(
        functools.partial(half_kernel, num, spare, bool(more)),
        out_shape=jax.ShapeDtypeStruct((kids, 2, height // 4, width), F32),
        in_specs=[pl.BlockSpec(memory_space=pltpu.SMEM)] + [pl.BlockSpec(memory_space=pltpu.VMEM)] * len(arrays),
        out_specs=pl.BlockSpec(memory_space=pltpu.VMEM),
        input_output_aliases={len(arrays): 0} if more else {},
        compiler_params=pltpu.CompilerParams(vmem_limit_bytes=16 * 2**20),
        cost_estimate=pl.CostEstimate(
            flops=weight * (num + len(spare)) * depth * height * kids * width,
            bytes_accessed=weight * num * depth * height,
            transcendentals=0,
        ),
        name="half_product",
    )(where, *arrays)


def pair_kernel(keep_ref, got_ref, parts_ref, rows_ref, message_ref):
    kids, halves, sub, width = keep_ref.shape
    last = parts_ref.shape[0] - 1
    for h in range(halves):
        for k in range(kids):
            both = jnp.dot(parts_ref[last, h], rows_ref[k], preferred_element_type=F32)
            both = both + (keep_ref[k, h] + got_ref[k, h])
            top = jnp.max(jnp.max(jnp.abs(both).reshape(-1, 8, width), axis=0), axis=(0, 1), keepdims=True)
            power = jnp.ceil(jnp.log2(jnp.maximum(top, 2.0**-100))) + 1.0
            message_ref[h * kids + k, :sub] = both * jnp.exp2(15.0 - power)
            message_ref[h * kids + k, sub:] = jnp.broadcast_to(power, (message_ref.shape[1] - sub, width))


def add_pair(keep, got, parts, rows):
    kids, halves, sub, width = keep.shape
    return pl.pallas_call(
        pair_kernel,
        out_shape=jax.ShapeDtypeStruct((kids * halves, sub + 16, width), F32),
        in_specs=[pl.BlockSpec(memory_space=pltpu.VMEM)] * 4,
        out_specs=pl.BlockSpec(memory_space=pltpu.VMEM),
        compiler_params=pltpu.CompilerParams(vmem_limit_bytes=16 * 2**20),
        cost_estimate=pl.CostEstimate(
            flops=2 * keep.size * parts.shape[3], bytes_accessed=3 * keep.nbytes, transcendentals=0
        ),
        name="add_pair",
    )(keep, got, parts, rows)


def shards(ancestor_cols, factor, block_mask, diag_inverse):
    num_z = lax.axis_size("z")
    num_y = lax.axis_size("y")
    quarter = ancestor_cols.shape[2]
    height = ancestor_cols.shape[3]
    width = factor.shape[2]
    sub = factor.shape[1]
    z = lax.axis_index("z")
    core = lax.axis_index("core")
    group = (lax.axis_index("xlo") * num_z + z) * 4 + lax.axis_index("xhi") * 2 + core
    blocks = ancestor_cols.reshape(2, num_z, quarter, height)

    order = [jnp.remainder(z + o, num_z) for o in (0, -1, 1, -2, 2, -3, 3, num_z // 2)]
    mine, theirs = [core], [1 - core]
    lists = [[group * (sub // width)], order[:7] + theirs, order[7:] + theirs, order + mine]
    places = jnp.stack(sum(lists, [])).astype(jnp.int32)
    ends = [sum(len(a) for a in lists[:n]) for n in range(len(lists) + 1)]
    place, first, given, every = (places[a:b] for a, b in zip(ends, ends[1:]))

    pieces, masked = mask(place, block_mask, factor, quarter)
    pieces, first, given, every = lax.optimization_barrier((pieces, first, given, every))
    own = lax.all_to_all(pieces.reshape(num_y * 2, quarter, width), ("y", "xlo"), 0, 0)
    own = own.reshape(num_y, 2 * quarter, width)

    up = [(i, (i + 1) % num_z) for i in range(num_z)]
    down = [(i, (i - 1) % num_z) for i in range(num_z)]
    below, above = lax.ppermute(own, "z", up), lax.ppermute(own, "z", down)
    below, turned = lax.optimization_barrier((below, turn(blocks)))
    below2, above2 = lax.ppermute(below, "z", up), lax.ppermute(above, "z", down)
    parts = lax.ppermute(pick(turned, given), "core", SWAP)
    below3, above3 = lax.ppermute(below2, "z", up), lax.ppermute(above2, "z", down)
    below3, parts = lax.optimization_barrier((below3, parts))
    far = lax.ppermute(below3, "z", up)

    near = [own, below, above, below2, above2, below3, above3]
    give = half_product(turned, first, near, weight=1)
    got = lax.ppermute(give, "core", SWAP)
    far_other = lax.ppermute(far, "core", SWAP)
    keep = half_product(turned, every, near + [far], weight=20)

    parts = lax.all_to_all(add_pair(keep, got, parts, far_other).astype(F16), ("xhi", "y"), 0, 0)
    back = jnp.exp2(parts[:, sub, 0].astype(F32) - 15.0)
    total = jnp.sum(parts[:, :sub].astype(F32) * back[:, None, None], 0)
    inverse_cols = lax.optimization_barrier((-total).astype(BF16))

    product = jnp.einsum("jw,jv->wv", masked, inverse_cols, preferred_element_type=F32)
    split = product.reshape(8, width // 8, width)
    mine = jnp.sum(lax.all_to_all(split, ALONG_X, 0, 0), 0)
    over_z = jnp.sum(lax.all_to_all(jnp.broadcast_to(mine, (num_z,) + mine.shape), "z", 0, 0), 0)
    whole = lax.all_to_all(jnp.broadcast_to(over_z, (8,) + over_z.shape), ALONG_X, 0, 0)
    return inverse_cols[None], diag_inverse - whole.reshape(1, width, width)


def solution(mesh):
    fine = Mesh(mesh.devices.reshape(4, 2, 8, 2, 2), AXES)
    rows = ROW + COL
    in_specs = (P(None, COL, "y", ROW), P("y", rows, None), P("y", None), P("y", None, None))
    out_specs = (P("y", rows, None), P("y", None, None))
    return jax.shard_map(shards, mesh=fine, in_specs=in_specs, out_specs=out_specs, check_vma=False)
```

```python
import functools

import jax
import jax.numpy as jnp
from jax import lax
from jax.experimental import pallas as pl
from jax.experimental.pallas import tpu as pltpu
from jax.sharding import Mesh, PartitionSpec as P

AXES = ("y", "xlo", "z", "xhi", "core")
ROW = ("xlo", "z")
COL = ("xhi", "core")
ALONG_X = ("xlo", "xhi", "core")
F32 = jnp.float32
F16 = jnp.float16
BF16 = jnp.bfloat16
SWAP = [(0, 1), (1, 0)]
def mask_kernel(place_ref, mask_ref, factor_ref, pieces_ref, masked_ref):
    pair, quarter = pieces_ref.shape[1:3]
    width = factor_ref.shape[2]
    for k in range(pieces_ref.shape[0]):
        block = place_ref[0] + k * quarter // width
        part = factor_ref[0, k * quarter : (k + 1) * quarter]
        part = jnp.where(mask_ref[0, block] != 0, part, jnp.zeros_like(part))
        masked_ref[k * quarter : (k + 1) * quarter] = part
        for x in range(pair):
            pieces_ref[k, x] = part


def mask(place, block_mask, factor, quarter):
    _, sub, width = factor.shape
    return pl.pallas_call(
        mask_kernel,
        out_shape=(
            jax.ShapeDtypeStruct((sub // quarter, 2, quarter, width), BF16),
            jax.ShapeDtypeStruct((sub, width), BF16),
        ),
        in_specs=[pl.BlockSpec(memory_space=pltpu.SMEM)] * 2 + [pl.BlockSpec(memory_space=pltpu.VMEM)],
        out_specs=tuple([pl.BlockSpec(memory_space=pltpu.VMEM)] * 2),
        cost_estimate=pl.CostEstimate(flops=factor.size, bytes_accessed=4 * factor.nbytes, transcendentals=0),
        name="mask",
    )(place, block_mask, factor)


def turn_kernel(cols_ref, out_ref):
    out_ref[0] = cols_ref[...].reshape(-1, cols_ref.shape[-1]).T


def turn(blocks):
    pair, num, quarter, height = blocks.shape
    tile = 512
    return pl.pallas_call(
        turn_kernel,
        out_shape=jax.ShapeDtypeStruct((num, height, pair * quarter), BF16),
        grid=(num, height // tile),
        in_specs=[pl.BlockSpec((pair, 1, quarter, tile), lambda z, i: (0, z, 0, i))],
        out_specs=pl.BlockSpec((1, tile, pair * quarter), lambda z, i: (z, i, 0)),
        compiler_params=pltpu.CompilerParams(vmem_limit_bytes=16 * 2**20),
        cost_estimate=pl.CostEstimate(flops=0, bytes_accessed=2 * blocks.nbytes, transcendentals=0),
        name="turn",
    )(blocks)


def rows_of(where_ref, half, sub):
    return pl.ds(pl.multiple_of((2 * half + where_ref[where_ref.shape[0] - 1]) * sub, sub), sub)


def pick_kernel(where_ref, turned_ref, out_ref):
    for b in range(out_ref.shape[0]):
        for h in range(2):
            out_ref[b, h] = turned_ref[where_ref[b], rows_of(where_ref, h, out_ref.shape[2])]


def pick(turned, where):
    _, height, depth = turned.shape
    num = where.shape[0] - 1
    return pl.pallas_call(
        pick_kernel,
        out_shape=jax.ShapeDtypeStruct((num, 2, height // 4, depth), BF16),
        in_specs=[pl.BlockSpec(memory_space=pltpu.SMEM), pl.BlockSpec(memory_space=pltpu.VMEM)],
        out_specs=pl.BlockSpec(memory_space=pltpu.VMEM),
        compiler_params=pltpu.CompilerParams(vmem_limit_bytes=16 * 2**20),
        cost_estimate=pl.CostEstimate(flops=0, bytes_accessed=2 * num * height * depth, transcendentals=0),
        name="pick",
    )(where, turned)


def half_kernel(num, spare, more, where_ref, turned_ref, *refs):
    rows, out_ref = refs[: num + len(spare)], refs[-1]
    parts_ref = refs[num + len(spare)] if spare else None
    kids, _, sub, _ = out_ref.shape
    for h in range(2):
        here = rows_of(where_ref, h, sub)
        cols = [turned_ref[where_ref[b], here] for b in range(num)] + [parts_ref[p, h] for p in spare]
        cols = jnp.concatenate(cols, 1)
        for k in range(kids):
            value = jnp.dot(cols, jnp.concatenate([r[k] for r in rows], 0), preferred_element_type=F32)
            out_ref[k, h] = refs[-2][k, h] + value if more else value


def half_product(turned, where, rows, partial=None, parts=None, spare=(), others=(), weight=1):
    num = len(rows)
    _, height, depth = turned.shape
    kids, _, width = rows[0].shape
    more = [] if partial is None else [partial]
    extra = [parts] if spare else []
    arrays = [turned, *rows, *others, *extra, *more]
    return pl.pallas_call(
        functools.partial(half_kernel, num, spare, bool(more)),
        out_shape=jax.ShapeDtypeStruct((kids, 2, height // 4, width), F32),
        in_specs=[pl.BlockSpec(memory_space=pltpu.SMEM)] + [pl.BlockSpec(memory_space=pltpu.VMEM)] * len(arrays),
        out_specs=pl.BlockSpec(memory_space=pltpu.VMEM),
        input_output_aliases={len(arrays): 0} if more else {},
        compiler_params=pltpu.CompilerParams(vmem_limit_bytes=16 * 2**20),
        cost_estimate=pl.CostEstimate(
            flops=weight * (num + len(spare)) * depth * height * kids * width,
            bytes_accessed=weight * num * depth * height,
            transcendentals=0,
        ),
        name="half_product",
    )(where, *arrays)


def pair_kernel(keep_ref, got_ref, parts_ref, rows_ref, message_ref):
    kids, halves, sub, width = keep_ref.shape
    last = parts_ref.shape[0] - 1
    for h in range(halves):
        for k in range(kids):
            both = jnp.dot(parts_ref[last, h], rows_ref[k], preferred_element_type=F32)
            both = both + (keep_ref[k, h] + got_ref[k, h])
            top = jnp.max(jnp.max(jnp.abs(both).reshape(-1, 8, width), axis=0), axis=(0, 1), keepdims=True)
            power = jnp.ceil(jnp.log2(jnp.maximum(top, 2.0**-100))) + 1.0
            message_ref[h * kids + k, :sub] = both * jnp.exp2(15.0 - power)
            message_ref[h * kids + k, sub:] = jnp.broadcast_to(power, (message_ref.shape[1] - sub, width))


def add_pair(keep, got, parts, rows):
    kids, halves, sub, width = keep.shape
    return pl.pallas_call(
        pair_kernel,
        out_shape=jax.ShapeDtypeStruct((kids * halves, sub + 16, width), F32),
        in_specs=[pl.BlockSpec(memory_space=pltpu.VMEM)] * 4,
        out_specs=pl.BlockSpec(memory_space=pltpu.VMEM),
        compiler_params=pltpu.CompilerParams(vmem_limit_bytes=16 * 2**20),
        cost_estimate=pl.CostEstimate(
            flops=2 * keep.size * parts.shape[3], bytes_accessed=3 * keep.nbytes, transcendentals=0
        ),
        name="add_pair",
    )(keep, got, parts, rows)


def shards(ancestor_cols, factor, block_mask, diag_inverse):
    num_z = lax.axis_size("z")
    num_y = lax.axis_size("y")
    quarter = ancestor_cols.shape[2]
    height = ancestor_cols.shape[3]
    width = factor.shape[2]
    sub = factor.shape[1]
    z = lax.axis_index("z")
    core = lax.axis_index("core")
    group = (lax.axis_index("xlo") * num_z + z) * 4 + lax.axis_index("xhi") * 2 + core
    blocks = ancestor_cols.reshape(2, num_z, quarter, height)

    order = [jnp.remainder(z + o, num_z) for o in (0, -1, 1, -2, 2, -3, 3, num_z // 2)]
    five, late, last, mine, theirs = order[:5], order[5:7], order[7:], [core], [1 - core]
    lists = [[group * (sub // width)], five + theirs, late + theirs, last + theirs, five + mine, late + last + mine]
    places = jnp.stack(sum(lists, [])).astype(jnp.int32)
    ends = [sum(len(a) for a in lists[:n]) for n in range(len(lists) + 1)]
    place, give5, give7, given, keep5, keep8 = (places[a:b] for a, b in zip(ends, ends[1:]))

    pieces, masked = mask(place, block_mask, factor, quarter)
    pieces, give5, give7, given, keep5, keep8 = lax.optimization_barrier((pieces, give5, give7, given, keep5, keep8))
    own = lax.all_to_all(pieces.reshape(num_y * 2, quarter, width), ("y", "xlo"), 0, 0)
    own = own.reshape(num_y, 2 * quarter, width)

    up = [(i, (i + 1) % num_z) for i in range(num_z)]
    down = [(i, (i - 1) % num_z) for i in range(num_z)]
    below, above = lax.ppermute(own, "z", up), lax.ppermute(own, "z", down)
    below, turned = lax.optimization_barrier((below, turn(blocks)))
    below2, above2 = lax.ppermute(below, "z", up), lax.ppermute(above, "z", down)
    parts = lax.ppermute(pick(turned, given), "core", SWAP)
    below3, above3 = lax.ppermute(below2, "z", up), lax.ppermute(above2, "z", down)
    near = [own, below, above, below2, above2]
    give = half_product(turned, give5, near, weight=10)
    keep = half_product(turned, keep5, near, weight=10)
    below3, parts, keep, give = lax.optimization_barrier((below3, parts, keep, give))
    far = lax.ppermute(below3, "z", up)

    give = half_product(turned, give7, [below3, above3], give)
    got = lax.ppermute(give, "core", SWAP)
    far_other = lax.ppermute(far, "core", SWAP)
    keep = half_product(turned, keep8, [below3, above3, far], keep, weight=60)

    parts = lax.all_to_all(add_pair(keep, got, parts, far_other).astype(F16), ("xhi", "y"), 0, 0)
    back = jnp.exp2(parts[:, sub, 0].astype(F32) - 15.0)
    total = jnp.sum(parts[:, :sub].astype(F32) * back[:, None, None], 0)
    inverse_cols = lax.optimization_barrier((-total).astype(BF16))

    product = jnp.einsum("jw,jv->wv", masked, inverse_cols, preferred_element_type=F32)
    split = product.reshape(8, width // 8, width)
    mine = jnp.sum(lax.all_to_all(split, ALONG_X, 0, 0), 0)
    over_z = jnp.sum(lax.all_to_all(jnp.broadcast_to(mine, (num_z,) + mine.shape), "z", 0, 0), 0)
    whole = lax.all_to_all(jnp.broadcast_to(over_z, (8,) + over_z.shape), ALONG_X, 0, 0)
    return inverse_cols[None], diag_inverse - whole.reshape(1, width, width)


def solution(mesh):
    fine = Mesh(mesh.devices.reshape(4, 2, 8, 2, 2), AXES)
    rows = ROW + COL
    in_specs = (P(None, COL, "y", ROW), P("y", rows, None), P("y", None), P("y", None, None))
    out_specs = (P("y", rows, None), P("y", None, None))
    return jax.shard_map(shards, mesh=fine, in_specs=in_specs, out_specs=out_specs, check_vma=False)
```

```python
import functools

import jax
import jax.numpy as jnp
from jax import lax
from jax.experimental import pallas as pl
from jax.experimental.pallas import tpu as pltpu
from jax.sharding import Mesh, PartitionSpec as P

AXES = ("y", "xlo", "z", "xhi", "core")
ROW = ("xlo", "z")
COL = ("xhi", "core")
ALONG_X = ("xlo", "xhi", "core")
F32 = jnp.float32
F16 = jnp.float16
BF16 = jnp.bfloat16
SWAP = [(0, 1), (1, 0)]
def mask_kernel(place_ref, mask_ref, factor_ref, pieces_ref, masked_ref):
    pair, quarter = pieces_ref.shape[1:3]
    width = factor_ref.shape[2]
    for k in range(pieces_ref.shape[0]):
        block = place_ref[0] + k * quarter // width
        part = factor_ref[0, k * quarter : (k + 1) * quarter]
        part = jnp.where(mask_ref[0, block] != 0, part, jnp.zeros_like(part))
        masked_ref[k * quarter : (k + 1) * quarter] = part
        for x in range(pair):
            pieces_ref[k, x] = part


def mask(place, block_mask, factor, quarter):
    _, sub, width = factor.shape
    return pl.pallas_call(
        mask_kernel,
        out_shape=(
            jax.ShapeDtypeStruct((sub // quarter, 2, quarter, width), BF16),
            jax.ShapeDtypeStruct((sub, width), BF16),
        ),
        in_specs=[pl.BlockSpec(memory_space=pltpu.SMEM)] * 2 + [pl.BlockSpec(memory_space=pltpu.VMEM)],
        out_specs=tuple([pl.BlockSpec(memory_space=pltpu.VMEM)] * 2),
        cost_estimate=pl.CostEstimate(flops=factor.size, bytes_accessed=4 * factor.nbytes, transcendentals=0),
        name="mask",
    )(place, block_mask, factor)


def turn_kernel(cols_ref, out_ref):
    out_ref[0] = cols_ref[...].reshape(-1, cols_ref.shape[-1]).T


def turn(blocks):
    pair, num, quarter, height = blocks.shape
    tile = 512
    return pl.pallas_call(
        turn_kernel,
        out_shape=jax.ShapeDtypeStruct((num, height, pair * quarter), BF16),
        grid=(num, height // tile),
        in_specs=[pl.BlockSpec((pair, 1, quarter, tile), lambda z, i: (0, z, 0, i))],
        out_specs=pl.BlockSpec((1, tile, pair * quarter), lambda z, i: (z, i, 0)),
        compiler_params=pltpu.CompilerParams(vmem_limit_bytes=16 * 2**20),
        cost_estimate=pl.CostEstimate(flops=0, bytes_accessed=2 * blocks.nbytes, transcendentals=0),
        name="turn",
    )(blocks)


def rows_of(where_ref, half, sub):
    return pl.ds(pl.multiple_of((2 * half + where_ref[where_ref.shape[0] - 1]) * sub, sub), sub)


def pick_kernel(where_ref, turned_ref, out_ref):
    for b in range(out_ref.shape[0]):
        for h in range(2):
            out_ref[b, h] = turned_ref[where_ref[b], rows_of(where_ref, h, out_ref.shape[2])]


def pick(turned, where):
    _, height, depth = turned.shape
    num = where.shape[0] - 1
    return pl.pallas_call(
        pick_kernel,
        out_shape=jax.ShapeDtypeStruct((num, 2, height // 4, depth), BF16),
        in_specs=[pl.BlockSpec(memory_space=pltpu.SMEM), pl.BlockSpec(memory_space=pltpu.VMEM)],
        out_specs=pl.BlockSpec(memory_space=pltpu.VMEM),
        compiler_params=pltpu.CompilerParams(vmem_limit_bytes=16 * 2**20),
        cost_estimate=pl.CostEstimate(flops=0, bytes_accessed=2 * num * height * depth, transcendentals=0),
        name="pick",
    )(where, turned)


def part_kernel(first, rows_ref, out_ref):
    out_ref[...] = rows_ref[first : first + out_ref.shape[0]]


def part(rows, first):
    return pl.pallas_call(
        functools.partial(part_kernel, first),
        out_shape=jax.ShapeDtypeStruct((rows.shape[0] // 2, *rows.shape[1:]), BF16),
        in_specs=[pl.BlockSpec(memory_space=pltpu.VMEM)],
        out_specs=pl.BlockSpec(memory_space=pltpu.VMEM),
        compiler_params=pltpu.CompilerParams(vmem_limit_bytes=16 * 2**20),
        cost_estimate=pl.CostEstimate(flops=0, bytes_accessed=0, transcendentals=0),
        name="part",
    )(rows)


def child(rows, k):
    for r in rows:
        if k < r.shape[0]:
            return r[k]
        k -= r.shape[0]


def half_kernel(num, split, more, where_ref, turned_ref, *refs):
    rows, out_ref = [[r] for r in refs[:num]], refs[-1]
    if split:
        rows[-1].append(refs[num])
    kids, _, sub, _ = out_ref.shape
    for h in range(2):
        here = rows_of(where_ref, h, sub)
        cols = [turned_ref[where_ref[b], here] for b in range(num)]
        cols = jnp.concatenate(cols, 1)
        for k in range(kids):
            value = jnp.dot(cols, jnp.concatenate([child(r, k) for r in rows], 0), preferred_element_type=F32)
            out_ref[k, h] = refs[-2][k, h] + value if more else value


def half_product(turned, where, rows, partial=None, split=0, weight=1):
    num = len(rows) - split
    _, height, depth = turned.shape
    kids, _, width = rows[0].shape
    more = [] if partial is None else [partial]
    arrays = [turned, *rows, *more]
    return pl.pallas_call(
        functools.partial(half_kernel, num, split, bool(more)),
        out_shape=jax.ShapeDtypeStruct((kids, 2, height // 4, width), F32),
        in_specs=[pl.BlockSpec(memory_space=pltpu.SMEM)] + [pl.BlockSpec(memory_space=pltpu.VMEM)] * len(arrays),
        out_specs=pl.BlockSpec(memory_space=pltpu.VMEM),
        input_output_aliases={len(arrays): 0} if more else {},
        compiler_params=pltpu.CompilerParams(vmem_limit_bytes=16 * 2**20),
        cost_estimate=pl.CostEstimate(
            flops=weight * num * depth * height * kids * width,
            bytes_accessed=weight * num * depth * height,
            transcendentals=0,
        ),
        name="half_product",
    )(where, *arrays)


def pair_kernel(keep_ref, got_ref, parts_ref, low_ref, high_ref, message_ref):
    kids, halves, sub, width = keep_ref.shape
    last = parts_ref.shape[0] - 1
    for h in range(halves):
        for k in range(kids):
            both = jnp.dot(parts_ref[last, h], child([low_ref, high_ref], k), preferred_element_type=F32)
            both = both + (keep_ref[k, h] + got_ref[k, h])
            top = jnp.max(jnp.max(jnp.abs(both).reshape(-1, 8, width), axis=0), axis=(0, 1), keepdims=True)
            power = jnp.ceil(jnp.log2(jnp.maximum(top, 2.0**-100))) + 1.0
            message_ref[h * kids + k, :sub] = both * jnp.exp2(15.0 - power)
            message_ref[h * kids + k, sub:] = jnp.broadcast_to(power, (message_ref.shape[1] - sub, width))


def add_pair(keep, got, parts, low, high):
    kids, halves, sub, width = keep.shape
    return pl.pallas_call(
        pair_kernel,
        out_shape=jax.ShapeDtypeStruct((kids * halves, sub + 16, width), F32),
        in_specs=[pl.BlockSpec(memory_space=pltpu.VMEM)] * 5,
        out_specs=pl.BlockSpec(memory_space=pltpu.VMEM),
        compiler_params=pltpu.CompilerParams(vmem_limit_bytes=16 * 2**20),
        cost_estimate=pl.CostEstimate(
            flops=2 * keep.size * parts.shape[3], bytes_accessed=3 * keep.nbytes, transcendentals=0
        ),
        name="add_pair",
    )(keep, got, parts, low, high)


def shards(ancestor_cols, factor, block_mask, diag_inverse):
    num_z = lax.axis_size("z")
    num_y = lax.axis_size("y")
    quarter = ancestor_cols.shape[2]
    height = ancestor_cols.shape[3]
    width = factor.shape[2]
    sub = factor.shape[1]
    z = lax.axis_index("z")
    core = lax.axis_index("core")
    group = (lax.axis_index("xlo") * num_z + z) * 4 + lax.axis_index("xhi") * 2 + core
    blocks = ancestor_cols.reshape(2, num_z, quarter, height)

    order = [jnp.remainder(z + o, num_z) for o in (0, -1, 1, -2, 2, -3, 3, num_z // 2)]
    five, late, last, mine, theirs = order[:5], order[5:7], order[7:], [core], [1 - core]
    lists = [[group * (sub // width)], five + theirs, late + theirs, last + theirs, five + mine, late + last + mine]
    places = jnp.stack(sum(lists, [])).astype(jnp.int32)
    ends = [sum(len(a) for a in lists[:n]) for n in range(len(lists) + 1)]
    place, give5, give7, given, keep5, keep8 = (places[a:b] for a, b in zip(ends, ends[1:]))

    pieces, masked = mask(place, block_mask, factor, quarter)
    pieces, give5, give7, given, keep5, keep8 = lax.optimization_barrier((pieces, give5, give7, given, keep5, keep8))
    own = lax.all_to_all(pieces.reshape(num_y * 2, quarter, width), ("y", "xlo"), 0, 0)
    own = own.reshape(num_y, 2 * quarter, width)

    up = [(i, (i + 1) % num_z) for i in range(num_z)]
    down = [(i, (i - 1) % num_z) for i in range(num_z)]
    below, above = lax.ppermute(own, "z", up), lax.ppermute(own, "z", down)
    below, turned = lax.optimization_barrier((below, turn(blocks)))
    below2, above2 = lax.ppermute(below, "z", up), lax.ppermute(above, "z", down)
    parts = lax.ppermute(pick(turned, given), "core", SWAP)
    below3, above3 = lax.ppermute(below2, "z", up), lax.ppermute(above2, "z", down)
    near = [own, below, above, below2, above2]
    give = half_product(turned, give5, near, weight=10)
    keep = half_product(turned, keep5, near, weight=10)
    below3, parts, keep, give = lax.optimization_barrier((below3, parts, keep, give))
    far = [lax.ppermute(part(below3, 0), "z", up), lax.ppermute(part(above3, num_y // 2), "z", down)]

    give = half_product(turned, give7, [below3, above3], give)
    got = lax.ppermute(give, "core", SWAP)
    other = [lax.ppermute(f, "core", SWAP) for f in far]
    keep = half_product(turned, keep8, [below3, above3, *far], keep, split=1, weight=60)

    parts = lax.all_to_all(add_pair(keep, got, parts, *other).astype(F16), ("xhi", "y"), 0, 0)
    back = jnp.exp2(parts[:, sub, 0].astype(F32) - 15.0)
    total = jnp.sum(parts[:, :sub].astype(F32) * back[:, None, None], 0)
    inverse_cols = lax.optimization_barrier((-total).astype(BF16))

    product = jnp.einsum("jw,jv->wv", masked, inverse_cols, preferred_element_type=F32)
    split = product.reshape(8, width // 8, width)
    mine = jnp.sum(lax.all_to_all(split, ALONG_X, 0, 0), 0)
    over_z = jnp.sum(lax.all_to_all(jnp.broadcast_to(mine, (num_z,) + mine.shape), "z", 0, 0), 0)
    whole = lax.all_to_all(jnp.broadcast_to(over_z, (8,) + over_z.shape), ALONG_X, 0, 0)
    return inverse_cols[None], diag_inverse - whole.reshape(1, width, width)


def solution(mesh):
    fine = Mesh(mesh.devices.reshape(4, 2, 8, 2, 2), AXES)
    rows = ROW + COL
    in_specs = (P(None, COL, "y", ROW), P("y", rows, None), P("y", None), P("y", None, None))
    out_specs = (P("y", rows, None), P("y", None, None))
    return jax.shard_map(shards, mesh=fine, in_specs=in_specs, out_specs=out_specs, check_vma=False)
```

```python
import functools

import jax
import jax.numpy as jnp
from jax import lax
from jax.experimental import pallas as pl
from jax.experimental.pallas import tpu as pltpu
from jax.sharding import Mesh, PartitionSpec as P

AXES = ("y", "xlo", "z", "xhi", "core")
ROW = ("xlo", "z")
COL = ("xhi", "core")
ALONG_X = ("xlo", "xhi", "core")
F32 = jnp.float32
F16 = jnp.float16
BF16 = jnp.bfloat16
SWAP = [(0, 1), (1, 0)]
def mask_kernel(place_ref, mask_ref, factor_ref, pieces_ref, masked_ref):
    pair, quarter = pieces_ref.shape[1:3]
    width = factor_ref.shape[2]
    for k in range(pieces_ref.shape[0]):
        block = place_ref[0] + k * quarter // width
        part = factor_ref[0, k * quarter : (k + 1) * quarter]
        part = jnp.where(mask_ref[0, block] != 0, part, jnp.zeros_like(part))
        masked_ref[k * quarter : (k + 1) * quarter] = part
        for x in range(pair):
            pieces_ref[k, x] = part


def mask(place, block_mask, factor, quarter):
    _, sub, width = factor.shape
    return pl.pallas_call(
        mask_kernel,
        out_shape=(
            jax.ShapeDtypeStruct((sub // quarter, 2, quarter, width), BF16),
            jax.ShapeDtypeStruct((sub, width), BF16),
        ),
        in_specs=[pl.BlockSpec(memory_space=pltpu.SMEM)] * 2 + [pl.BlockSpec(memory_space=pltpu.VMEM)],
        out_specs=tuple([pl.BlockSpec(memory_space=pltpu.VMEM)] * 2),
        cost_estimate=pl.CostEstimate(flops=factor.size, bytes_accessed=4 * factor.nbytes, transcendentals=0),
        name="mask",
    )(place, block_mask, factor)


def turn_kernel(cols_ref, out_ref):
    out_ref[0] = cols_ref[...].reshape(-1, cols_ref.shape[-1]).T


def turn(blocks):
    pair, num, quarter, height = blocks.shape
    tile = 512
    return pl.pallas_call(
        turn_kernel,
        out_shape=jax.ShapeDtypeStruct((num, height, pair * quarter), BF16),
        grid=(num, height // tile),
        in_specs=[pl.BlockSpec((pair, 1, quarter, tile), lambda z, i: (0, z, 0, i))],
        out_specs=pl.BlockSpec((1, tile, pair * quarter), lambda z, i: (z, i, 0)),
        compiler_params=pltpu.CompilerParams(vmem_limit_bytes=16 * 2**20),
        cost_estimate=pl.CostEstimate(flops=0, bytes_accessed=2 * blocks.nbytes, transcendentals=0),
        name="turn",
    )(blocks)


def rows_of(where_ref, half, sub):
    return pl.ds(pl.multiple_of((2 * half + where_ref[where_ref.shape[0] - 1]) * sub, sub), sub)


def pick_kernel(where_ref, turned_ref, out_ref):
    for b in range(out_ref.shape[0]):
        for h in range(2):
            out_ref[b, h] = turned_ref[where_ref[b], rows_of(where_ref, h, out_ref.shape[2])]


def pick(turned, where):
    _, height, depth = turned.shape
    num = where.shape[0] - 1
    return pl.pallas_call(
        pick_kernel,
        out_shape=jax.ShapeDtypeStruct((num, 2, height // 4, depth), BF16),
        in_specs=[pl.BlockSpec(memory_space=pltpu.SMEM), pl.BlockSpec(memory_space=pltpu.VMEM)],
        out_specs=pl.BlockSpec(memory_space=pltpu.VMEM),
        compiler_params=pltpu.CompilerParams(vmem_limit_bytes=16 * 2**20),
        cost_estimate=pl.CostEstimate(flops=0, bytes_accessed=2 * num * height * depth, transcendentals=0),
        name="pick",
    )(where, turned)


def half_kernel(num, spare, more, where_ref, turned_ref, *refs):
    rows, out_ref = refs[: num + len(spare)], refs[-1]
    parts_ref = refs[num + len(spare)] if spare else None
    kids, _, sub, _ = out_ref.shape
    for h in range(2):
        here = rows_of(where_ref, h, sub)
        cols = [turned_ref[where_ref[b], here] for b in range(num)] + [parts_ref[p, h] for p in spare]
        cols = jnp.concatenate(cols, 1)
        for k in range(kids):
            value = jnp.dot(cols, jnp.concatenate([r[k] for r in rows], 0), preferred_element_type=F32)
            out_ref[k, h] = refs[-2][k, h] + value if more else value


def half_product(turned, where, rows, partial=None, parts=None, spare=(), others=(), weight=1):
    num = len(rows)
    _, height, depth = turned.shape
    kids, _, width = rows[0].shape
    more = [] if partial is None else [partial]
    extra = [parts] if spare else []
    arrays = [turned, *rows, *others, *extra, *more]
    return pl.pallas_call(
        functools.partial(half_kernel, num, spare, bool(more)),
        out_shape=jax.ShapeDtypeStruct((kids, 2, height // 4, width), F32),
        in_specs=[pl.BlockSpec(memory_space=pltpu.SMEM)] + [pl.BlockSpec(memory_space=pltpu.VMEM)] * len(arrays),
        out_specs=pl.BlockSpec(memory_space=pltpu.VMEM),
        input_output_aliases={len(arrays): 0} if more else {},
        compiler_params=pltpu.CompilerParams(vmem_limit_bytes=16 * 2**20),
        cost_estimate=pl.CostEstimate(
            flops=weight * (num + len(spare)) * depth * height * kids * width,
            bytes_accessed=weight * num * depth * height,
            transcendentals=0,
        ),
        name="half_product",
    )(where, *arrays)


def pair_kernel(keep_ref, got_ref, parts_ref, rows_ref, message_ref):
    kids, halves, sub, width = keep_ref.shape
    last = parts_ref.shape[0] - 1
    for h in range(halves):
        for k in range(kids):
            both = jnp.dot(parts_ref[last, h], rows_ref[k], preferred_element_type=F32)
            both = both + (keep_ref[k, h] + got_ref[k, h])
            top = jnp.max(jnp.max(jnp.abs(both).reshape(-1, 8, width), axis=0), axis=(0, 1), keepdims=True)
            power = jnp.ceil(jnp.log2(jnp.maximum(top, 2.0**-100))) + 1.0
            message_ref[h * kids + k, :sub] = both * jnp.exp2(15.0 - power)
            message_ref[h * kids + k, sub:] = jnp.broadcast_to(power, (message_ref.shape[1] - sub, width))


def add_pair(keep, got, parts, rows):
    kids, halves, sub, width = keep.shape
    return pl.pallas_call(
        pair_kernel,
        out_shape=jax.ShapeDtypeStruct((kids * halves, sub + 16, width), F32),
        in_specs=[pl.BlockSpec(memory_space=pltpu.VMEM)] * 4,
        out_specs=pl.BlockSpec(memory_space=pltpu.VMEM),
        compiler_params=pltpu.CompilerParams(vmem_limit_bytes=16 * 2**20),
        cost_estimate=pl.CostEstimate(
            flops=2 * keep.size * parts.shape[3], bytes_accessed=3 * keep.nbytes, transcendentals=0
        ),
        name="add_pair",
    )(keep, got, parts, rows)


def shards(ancestor_cols, factor, block_mask, diag_inverse):
    num_z = lax.axis_size("z")
    num_y = lax.axis_size("y")
    quarter = ancestor_cols.shape[2]
    height = ancestor_cols.shape[3]
    width = factor.shape[2]
    sub = factor.shape[1]
    z = lax.axis_index("z")
    core = lax.axis_index("core")
    group = (lax.axis_index("xlo") * num_z + z) * 4 + lax.axis_index("xhi") * 2 + core
    blocks = ancestor_cols.reshape(2, num_z, quarter, height)

    order = [jnp.remainder(z + o, num_z) for o in (0, -1, 1, -2, 2, -3, 3, num_z // 2)]
    five, late, last, mine, theirs = order[:5], order[5:7], order[7:], [core], [1 - core]
    lists = [[group * (sub // width)], five + theirs, late + theirs, last + theirs, five + mine, late + last + mine]
    places = jnp.stack(sum(lists, [])).astype(jnp.int32)
    ends = [sum(len(a) for a in lists[:n]) for n in range(len(lists) + 1)]
    place, give5, give7, given, keep5, keep8 = (places[a:b] for a, b in zip(ends, ends[1:]))

    pieces, masked = mask(place, block_mask, factor, quarter)
    pieces, give5, give7, given, keep5, keep8 = lax.optimization_barrier((pieces, give5, give7, given, keep5, keep8))
    own = lax.all_to_all(pieces.reshape(num_y * 2, quarter, width), ("y", "xlo"), 0, 0)
    own = own.reshape(num_y, 2 * quarter, width)

    up = [(i, (i + 1) % num_z) for i in range(num_z)]
    down = [(i, (i - 1) % num_z) for i in range(num_z)]
    below, above = lax.ppermute(own, "z", up), lax.ppermute(own, "z", down)
    below, turned = lax.optimization_barrier((below, turn(blocks)))
    below2, above2 = lax.ppermute(below, "z", up), lax.ppermute(above, "z", down)
    parts = lax.ppermute(pick(turned, given), "core", SWAP)
    below3, above3 = lax.ppermute(below2, "z", up), lax.ppermute(above2, "z", down)
    near = [own, below, above, below2, above2]
    give = half_product(turned, give5, near, weight=10)
    keep = half_product(turned, keep5, near, weight=10)
    below3, parts, keep, give = lax.optimization_barrier((below3, parts, keep, give))
    far = lax.ppermute(below3, "z", up)

    give = half_product(turned, give7, [below3, above3], give)
    got = lax.ppermute(give, "core", SWAP)
    far_other = lax.ppermute(far, "core", SWAP)
    keep = half_product(turned, keep8, [below3, above3, far], keep, weight=60)

    parts = lax.all_to_all(add_pair(keep, got, parts, far_other).astype(F16), ("xhi", "y"), 0, 0)
    back = jnp.exp2(parts[:, sub, 0].astype(F32) - 15.0)
    total = jnp.sum(parts[:, :sub].astype(F32) * back[:, None, None], 0)
    inverse_cols = lax.optimization_barrier((-total).astype(BF16))

    product = jnp.einsum("jw,jv->wv", masked, inverse_cols, preferred_element_type=F32)
    halves = product.reshape(2, width // 2, width)
    mine = lax.dynamic_index_in_dim(halves, core, 0, keepdims=False)
    give = lax.dynamic_index_in_dim(halves, 1 - core, 0, keepdims=False)
    mine = mine + lax.ppermute(give, "core", SWAP)
    mine = jnp.sum(lax.all_to_all(mine.reshape(4, width // 8, width), ("xlo", "xhi"), 0, 0), 0)
    over_z = jnp.sum(lax.all_to_all(jnp.broadcast_to(mine, (num_z,) + mine.shape), "z", 0, 0), 0)
    half = lax.all_to_all(jnp.broadcast_to(over_z, (4,) + over_z.shape), ("xlo", "xhi"), 0, 0)
    half = half.reshape(width // 2, width)
    rest = lax.ppermute(half, "core", SWAP)
    whole = jnp.where(core == 0, jnp.concatenate([half, rest], 0), jnp.concatenate([rest, half], 0))
    return inverse_cols[None], diag_inverse - whole.reshape(1, width, width)


def solution(mesh):
    fine = Mesh(mesh.devices.reshape(4, 2, 8, 2, 2), AXES)
    rows = ROW + COL
    in_specs = (P(None, COL, "y", ROW), P("y", rows, None), P("y", None), P("y", None, None))
    out_specs = (P("y", rows, None), P("y", None, None))
    return jax.shard_map(shards, mesh=fine, in_specs=in_specs, out_specs=out_specs, check_vma=False)
```
